32 devices in a mesh: dp: 4 (over z), tensor: 8 (over y, x, core).
Axes of the slice: x: 2, y: 2, z: 4, core: 2. Of those that a mesh axis runs over, the one named last changes fastest.
Arguments:
- residues: bfloat16 [2048, 1024], P('dp'), may hold values from -40 to 40
- block_protein: int32 [16], P('dp'), may hold values from 0 to 15, as said below
- protein_length: int32 [16], replicated, may hold values from 0 to 256, as said below
- decoder_group: int32 [16], replicated, may hold values from 0 to 3, as said below
- enc_gain: float32 [1024], replicated, may hold values from 0.1 to 1.9
- enc_query: bfloat16 [1024, 8192], P(None, 'tensor'), may hold values from -2 to 2
- enc_key: bfloat16 [1024, 8192], P(None, 'tensor'), may hold values from -2 to 2
- enc_value: bfloat16 [1024, 8192], P(None, 'tensor'), may hold values from -0.1875 to 0.1875
- enc_out: bfloat16 [8192, 1024], P('tensor'), may hold values from -0.1875 to 0.1875
- decoder_states: bfloat16 [1536, 1024], P('dp'), may hold values from -40 to 40
- query_protein: int32 [1536], P('dp'), may hold values from 0 to 15, as said below
- dec_gain: float32 [1024], replicated, may hold values from 0.1 to 1.9
- final_gain: float32 [1024], replicated, may hold values from 0.1 to 1.9
- cross_query: bfloat16 [1024, 8192], P(None, 'tensor'), may hold values from -2 to 2
- cross_key: bfloat16 [1024, 8192], P(None, 'tensor'), may hold values from -2 to 2
- cross_value: bfloat16 [1024, 8192], P(None, 'tensor'), may hold values from -0.1875 to 0.1875
- cross_out: bfloat16 [8192, 1024], P('tensor'), may hold values from -0.1875 to 0.1875
Outputs:
- encoded: bfloat16 [2048, 1024], P('dp', 'tensor')
- decoded: bfloat16 [1536, 1024], P(('dp', 'tensor'))
The draws below stay inside these ranges and needn't reach their ends.
Inputs may be any that keep to these rules, and one draw needn't show every extreme that they name: `block_protein`: block b of dp group d names a protein id from d * 4 to (d + 1) * 4 - 1; the blocks of one protein are consecutive and the ids rise along a group's blocks. `protein_length`: A protein of n blocks has a length from (n - 1) * 128 + 1 to n * 128; an id that no block names has length 0; no protein spans more than 2 blocks. `decoder_group`: at most 2 blocks of one dp group belong to proteins of one decoder group, and in every draw some decoder group gets exactly 2 blocks from every dp group; every decoder group owns a protein of positive length. `query_protein`: query row i names a protein of positive length whose decoder group is i // 384.
All inputs are finite; a program needn't handle non-finite values.
Results may differ from the reference program's by a relative error of at most 0.017.
Values may be sent and summed in bfloat16 or wider, within the bound.
A program may use at most 128 MiB of HBM per device.

```python
import jax
import jax.numpy as jnp
from jax import lax

D = 1024
HEAD_DIM = 128
BLOCK = 128
BLK_DEV = 4
Q_DEV = 384
HEADS = 64
SLOTS = 2
TOKENS = 2048
QROWS = 1536
PROTEINS = 16
N_DP = 4


def layout(key):
    base = jax.random.fold_in(key, 101)
    hot = jax.random.randint(jax.random.fold_in(base, 1), (), 0, N_DP)
    flip = jax.random.randint(jax.random.fold_in(base, 2), (N_DP,), 0, 2)
    cuts = jax.random.randint(jax.random.fold_in(base, 3), (N_DP, BLK_DEV), 0, 2)
    column = jnp.arange(BLK_DEV, dtype=jnp.int32)
    device = jnp.arange(N_DP, dtype=jnp.int32)[:, None]
    joined = (device == 0) & (column[None, :] < SLOTS)
    starts = jnp.where((column[None, :] == 0) | (column[None, :] == SLOTS), 1, jnp.where(joined, 0, cuts))
    local = jnp.cumsum(starts, axis=1).astype(jnp.int32) - 1
    block_ids = device * BLK_DEV + local
    in_hot = (column[None, :] < SLOTS) == (flip[:, None] == 0)
    other_start = jnp.where(flip == 0, SLOTS, 0)
    first_local = jnp.sum(jnp.where(column[None, :] == other_start[:, None], local, 0), axis=1)
    random_pick = jax.random.randint(jax.random.fold_in(base, 4), (N_DP, BLK_DEV), 0, N_DP - 1)
    picked = jnp.take_along_axis(random_pick, local, axis=1)
    spread = jnp.where(local == first_local[:, None], device % (N_DP - 1), picked)
    dest = jnp.where(in_hot, hot, (hot + 1 + spread) % N_DP)
    target = jnp.arange(BLK_DEV, dtype=jnp.int32)
    match = local[:, None, :] == target[None, :, None]
    present = jnp.any(match, axis=2)
    owned = jnp.sum(match.astype(jnp.int32), axis=2)
    group_of = jnp.max(jnp.where(match, dest[:, None, :], -1), axis=2)
    filler = jax.random.randint(jax.random.fold_in(base, 5), (N_DP, BLK_DEV), 0, N_DP)
    groups = jnp.where(present, group_of, filler).reshape(-1)
    tail = jax.random.randint(jax.random.fold_in(base, 6), (N_DP, BLK_DEV), 1, BLOCK + 1)
    full_one = (device == 0) & (target[None, :] == 0)
    tail = jnp.where(full_one, BLOCK, tail)
    lengths = jnp.where(present, (owned - 1) * BLOCK + tail, 0).reshape(-1)
    candidate = (groups[None, :] == jnp.arange(N_DP, dtype=jnp.int32)[:, None]) & (lengths[None, :] > 0)
    counted = jnp.sum(candidate.astype(jnp.int32), axis=1)
    row_group = jnp.arange(QROWS, dtype=jnp.int32) // Q_DEV
    choose = jax.random.randint(jax.random.fold_in(base, 7), (QROWS,), 0, counted[row_group])
    running = jnp.cumsum(candidate.astype(jnp.int32), axis=1)
    select = candidate[row_group] & (running[row_group] == choose[:, None] + 1)
    ids = jnp.arange(PROTEINS, dtype=jnp.int32)
    queries = jnp.sum(jnp.where(select, ids[None, :], 0), axis=1).astype(jnp.int32)
    return (block_ids.reshape(-1).astype(jnp.int32), lengths.astype(jnp.int32), groups.astype(jnp.int32), queries)


def draw_block_protein(key, part):
    return layout(key)[0]


def draw_protein_length(key, part):
    return layout(key)[1]


def draw_decoder_group(key, part):
    return layout(key)[2]


def draw_query_protein(key, part):
    return layout(key)[3]


def states_draw(key, salt, rows):
    noise = jax.random.normal(jax.random.fold_in(key, salt), (rows, D), jnp.float32)
    return noise.astype(jnp.bfloat16)


def draw_residues(key, part):
    return states_draw(key, 31, TOKENS)


def draw_decoder_states(key, part):
    return states_draw(key, 41, QROWS)


def projection(key, salt, second):
    shape = (D, HEADS * HEAD_DIM)
    return jnp.clip(jax.random.normal(jax.random.fold_in(key, salt + 10 + second), shape, jnp.float32) * D ** (-0.5), -1.9, 1.9).astype(jnp.bfloat16)


def draw_enc_query(key, part):
    return projection(key, 200, 0)


def draw_enc_key(key, part):
    return projection(key, 200, 1)


def draw_cross_query(key, part):
    return projection(key, 300, 0)


def draw_cross_key(key, part):
    return projection(key, 300, 1)


def shard_levels(stream_key, extent, shards, low, high):
    def one(axis_at, shards_of):
        heights = jax.random.uniform(jax.random.fold_in(jax.random.fold_in(stream_key, 6), axis_at), (shards_of,), jnp.float32, low / len(shards), high / len(shards))
        return jnp.repeat(jnp.exp(heights), extent[axis_at] // shards_of).reshape((-1,) + (1,) * (len(extent) - axis_at - 1))

    level = one(*shards[0])
    for cut in shards[1:]:
        level = level * one(*cut)
    return level


def centred(key, extent, deviation, limit, split=(), kind=jnp.bfloat16):
    entries = deviation * jax.random.normal(key, extent, jnp.float32)
    if split:
        entries = entries * shard_levels(key, extent, split, -0.22, 0.18)
    return jnp.clip(entries, -limit, limit).astype(kind)


def setup_inputs(seed: int = 0) -> dict:
    arg_keys = jax.random.split(jax.random.key(seed), 18)
    return {
        "residues": draw_residues(jax.random.fold_in(arg_keys[17], 71), 0),
        "block_protein": draw_block_protein(jax.random.fold_in(arg_keys[17], 71), 0),
        "protein_length": draw_protein_length(jax.random.fold_in(arg_keys[17], 71), 0),
        "decoder_group": draw_decoder_group(jax.random.fold_in(arg_keys[17], 71), 0),
        "enc_gain": jnp.clip(1.0 + 0.18 * jax.random.normal(arg_keys[4], (D,), jnp.float32), 0.1, 1.9),
        "enc_query": draw_enc_query(jax.random.fold_in(arg_keys[17], 71), 0),
        "enc_key": draw_enc_key(jax.random.fold_in(arg_keys[17], 71), 0),
        "enc_value": centred(arg_keys[7], (D, HEADS * HEAD_DIM), D ** -0.5, 0.1875, ((1, 8),)),
        "enc_out": centred(arg_keys[8], (HEADS * HEAD_DIM, D), (8 * HEAD_DIM) ** -0.5, 0.1875, ((0, 8),)),
        "decoder_states": draw_decoder_states(jax.random.fold_in(arg_keys[17], 71), 0),
        "query_protein": draw_query_protein(jax.random.fold_in(arg_keys[17], 71), 0),
        "dec_gain": jnp.clip(1.0 + 0.18 * jax.random.normal(arg_keys[11], (D,), jnp.float32), 0.1, 1.9),
        "final_gain": jnp.clip(1.0 + 0.18 * jax.random.normal(arg_keys[12], (D,), jnp.float32), 0.1, 1.9),
        "cross_query": draw_cross_query(jax.random.fold_in(arg_keys[17], 71), 0),
        "cross_key": draw_cross_key(jax.random.fold_in(arg_keys[17], 71), 0),
        "cross_value": centred(arg_keys[15], (D, HEADS * HEAD_DIM), D ** -0.5, 0.1875, ((1, 8),)),
        "cross_out": centred(arg_keys[16], (HEADS * HEAD_DIM, D), (8 * HEAD_DIM) ** -0.5, 0.1875, ((0, 8),)),
    }


EPSILON = 1e-06
MASKED = -1000000000.0

def row_scale(matrix):
    values = matrix.astype(jnp.float32)
    return lax.rsqrt(lax.optimization_barrier(jnp.mean(values * values, axis=1, keepdims=True)) + EPSILON)

def attend(queries, keys, values, allowed):
    heads = queries.shape[1] // HEAD_DIM

    def by_head(matrix):
        return jnp.transpose(matrix.reshape(matrix.shape[0], heads, HEAD_DIM), (1, 0, 2))

    def one_head(item):
        head_queries, head_keys, head_values = item
        scores = jnp.dot(head_queries, jnp.transpose(head_keys), preferred_element_type=jnp.float32) * HEAD_DIM ** (-0.5)
        scores = jnp.where(allowed, scores, MASKED)
        top = lax.optimization_barrier(jnp.max(scores, axis=1, keepdims=True))
        expo = jnp.exp(scores - top)
        total = lax.optimization_barrier(jnp.sum(expo, axis=1, keepdims=True))
        weights = expo.astype(jnp.bfloat16)
        return jnp.dot(weights, head_values, preferred_element_type=jnp.float32) / total
    context = lax.map(one_head, (by_head(queries), by_head(keys), by_head(values)))
    return jnp.transpose(context, (1, 0, 2)).reshape(queries.shape[0], heads * HEAD_DIM).astype(jnp.bfloat16)

def token_layout(block_protein, protein_length):
    count = block_protein.shape[0]
    order = jnp.arange(count, dtype=jnp.int32)
    same = block_protein[:, None] == block_protein[None, :]
    offset = lax.optimization_barrier(jnp.sum(same & (order[None, :] < order[:, None]), axis=1)).astype(jnp.int32)
    live = jnp.clip(protein_length[block_protein] - offset * BLOCK, 0, BLOCK)
    position = jnp.arange(BLOCK, dtype=jnp.int32)
    valid = (position[None, :] < live[:, None]).reshape(-1)
    owner = jnp.repeat(block_protein, BLOCK)
    return (owner, valid)

def reference(residues, block_protein, protein_length, decoder_group, enc_gain, enc_query, enc_key, enc_value, enc_out, decoder_states, query_protein, dec_gain, final_gain, cross_query, cross_key, cross_value, cross_out):
    owner, valid = token_layout(block_protein, protein_length)
    normed = (residues.astype(jnp.float32) * row_scale(residues) * enc_gain[None, :]).astype(jnp.bfloat16)
    enc_q = jnp.dot(normed, enc_query, preferred_element_type=jnp.float32).astype(jnp.bfloat16)
    enc_k = jnp.dot(normed, enc_key, preferred_element_type=jnp.float32).astype(jnp.bfloat16)
    enc_v = jnp.dot(normed, enc_value, preferred_element_type=jnp.float32).astype(jnp.bfloat16)
    allowed = (owner[:, None] == owner[None, :]) & valid[None, :]
    context = attend(enc_q, enc_k, enc_v, allowed)
    encoded = (residues.astype(jnp.float32) + jnp.dot(context, enc_out, preferred_element_type=jnp.float32)).astype(jnp.bfloat16)
    scaled = (encoded.astype(jnp.float32) * final_gain[None, :]).astype(jnp.bfloat16)
    key_scale = row_scale(encoded)
    cross_k = (jnp.dot(scaled, cross_key, preferred_element_type=jnp.float32) * key_scale).astype(jnp.bfloat16)
    cross_v = (jnp.dot(scaled, cross_value, preferred_element_type=jnp.float32) * key_scale).astype(jnp.bfloat16)
    dec_normed = (decoder_states.astype(jnp.float32) * row_scale(decoder_states) * dec_gain[None, :]).astype(jnp.bfloat16)
    cross_q = jnp.dot(dec_normed, cross_query, preferred_element_type=jnp.float32).astype(jnp.bfloat16)
    owner_group = decoder_group[owner]
    query_group = (jnp.arange(decoder_states.shape[0], dtype=jnp.int32) // Q_DEV).astype(jnp.int32)
    cross_allowed = (query_protein[:, None] == owner[None, :]) & valid[None, :] & (owner_group[None, :] == query_group[:, None])
    cross_context = attend(cross_q, cross_k, cross_v, cross_allowed)
    decoded = (decoder_states.astype(jnp.float32) + jnp.dot(cross_context, cross_out, preferred_element_type=jnp.float32)).astype(jnp.bfloat16)
    return (encoded, decoded)
```

```python
import functools

import jax
import jax.numpy as jnp
from jax import lax
from jax.experimental import pallas as pl
from jax.experimental.pallas import tpu as pltpu
from jax.sharding import PartitionSpec as P

HEAD_DIM = 128
BLOCK = 128
LANES = 128

EPSILON = 1e-06
LOG2E = 1.4426950408889634
MASKED = -1000000000.0
SCORE_SCALE = HEAD_DIM ** (-0.5)
RAW_MASKED = MASKED / SCORE_SCALE
MESH = pl.DeviceIdType.MESH
F32 = jnp.float32
BF16 = jnp.bfloat16


def normalise(source, gain, target, rows):
    for start in range(0, source.shape[0], rows):
        values = source[start : start + rows, :].astype(F32)
        scale = lax.rsqrt(jnp.mean(values * values, axis=1, keepdims=True) + EPSILON)
        target[start : start + rows, :] = (values * scale * gain[...]).astype(BF16)


def project(source, weight, target, tile=256):
    @pl.loop(0, weight.shape[1] // tile)
    def _(index):
        columns = pl.ds(pl.multiple_of(index * tile, tile), tile)
        target[:, columns] = jnp.dot(
            source[...], weight[:, columns], preferred_element_type=F32
        ).astype(BF16)


def attend(queries, keys, values, bias, context, q_rows, k_rows, heads, together=2):
    @pl.loop(0, heads // together)
    def _(index):
        for inner in range(together):
            start = pl.multiple_of((index * together + inner) * HEAD_DIM, HEAD_DIM)
            columns = pl.ds(start, HEAD_DIM)
            scores = lax.dot_general(
                queries[q_rows, columns],
                keys[k_rows, columns],
                (((1,), (1,)), ((), ())),
                preferred_element_type=F32,
            )
            scores = scores + bias[...]
            top = jnp.max(scores, axis=1, keepdims=True)
            expo = jnp.exp2((scores - top) * (SCORE_SCALE * LOG2E))
            total = jnp.sum(expo, axis=1, keepdims=True)
            mixed = jnp.dot(
                expo.astype(BF16), values[k_rows, columns], preferred_element_type=F32
            )
            context[q_rows, columns] = (mixed / total).astype(BF16)


def kernel(
    groups,
    tensors,
    residues,
    block_protein,
    protein_length,
    decoder_group,
    enc_gain,
    enc_query,
    enc_key,
    enc_value,
    enc_out,
    decoder_states,
    query_protein,
    dec_gain,
    final_gain,
    cross_query,
    cross_key,
    cross_value,
    cross_out,
    encoded,
    decoded,
    res_v,
    dec_v,
    w_eq,
    w_ek,
    w_ev,
    w_eo,
    w_cq,
    w_ck,
    w_cv,
    w_co,
    normed,
    e_q,
    e_k,
    e_v,
    e_ctx,
    e_bias,
    part,
    rx1,
    tx2,
    rx2,
    placed,
    gath,
    meta_tx,
    meta_rx,
    d_normed,
    c_q,
    c_k,
    c_v,
    c_ctx,
    c_bias,
    scaled,
    dpart,
    drx1,
    dtx2,
    drx2,
    load_sem,
    meta_sem,
    rs1_sem,
    rs2_sem,
    a2a_sem,
    ag_sem,
    agp_sem,
    drs1_sem,
    drs2_sem,
):
    me_dp = lax.axis_index("dp")
    me_t = lax.axis_index("tensor")
    pairs = tensors // 2
    pair = me_t // 2
    side = lax.rem(me_t, 2)
    partner = pair * 2 + (1 - side)
    tok_rows, width = res_v.shape
    blocks = tok_rows // BLOCK
    slots = blocks // 2
    heads = e_q.shape[1] // HEAD_DIM
    half = tok_rows // 2
    half_blocks = blocks // 2
    share = encoded.shape[1]
    query_rows = dec_v.shape[0]
    row_share = query_rows // tensors
    row_pad = dpart.shape[3]

    def peer(step):
        return lax.rem(pair + step, pairs) * 2 + side

    loads = []
    for index, (src, dst) in enumerate(
        (
            (residues, res_v),
            (enc_query, w_eq),
            (enc_key, w_ek),
            (enc_value, w_ev),
            (enc_out, w_eo),
            (decoder_states, dec_v),
            (cross_query, w_cq),
            (cross_key, w_ck),
            (cross_value, w_cv),
            (cross_out, w_co),
        )
    ):
        load = pltpu.make_async_copy(src, dst, load_sem.at[index])
        load.start()
        loads.append(load)

    barrier = pltpu.get_barrier_semaphore()
    pl.semaphore_signal(barrier, inc=1, device_id={"tensor": partner}, device_id_type=MESH)
    for step in range(1, pairs):
        pl.semaphore_signal(
            barrier, inc=1, device_id={"tensor": peer(step)}, device_id_type=MESH
        )
    for step in range(1, groups):
        pl.semaphore_signal(
            barrier,
            inc=1,
            device_id={"dp": lax.rem(me_dp + step, groups)},
            device_id_type=MESH,
        )

    sent = []

    def send(src, dst, sems, device):
        copy = pltpu.make_async_remote_copy(
            src_ref=src,
            dst_ref=dst,
            send_sem=sems[0],
            recv_sem=sems[1],
            device_id=device,
            device_id_type=MESH,
        )
        copy.start()
        sent.append(copy)

    def arrive(dst, sems, device):
        pltpu.make_async_remote_copy(
            src_ref=dst,
            dst_ref=dst,
            send_sem=sems[0],
            recv_sem=sems[1],
            device_id=device,
            device_id_type=MESH,
        ).wait_recv()

    owner = [block_protein[b] for b in range(blocks)]
    live, dest, rank = [], [], []
    for b in range(blocks):
        offset = jnp.int32(0)
        for other in range(b):
            offset = offset + jnp.where(owner[other] == owner[b], 1, 0)
        length = protein_length[owner[b]]
        live.append(jnp.clip(length - offset * BLOCK, 0, BLOCK))
        dest.append(decoder_group[owner[b]])
    for b in range(blocks):
        place = jnp.int32(0)
        for other in range(b):
            place = place + jnp.where(dest[other] == dest[b], 1, 0)
        rank.append(place)

    lane = lax.broadcasted_iota(jnp.int32, (8, LANES), 1)
    row = lax.broadcasted_iota(jnp.int32, (8, LANES), 0)
    for g in range(groups):
        ids = jnp.full((8, LANES), -1, jnp.int32)
        for s in range(slots):
            slot_id, slot_live = jnp.int32(-1), jnp.int32(0)
            for b in range(blocks):
                match = (dest[b] == g) & (rank[b] == s)
                slot_id = jnp.where(match, owner[b], slot_id)
                slot_live = jnp.where(match, live[b], slot_live)
            row_live = jnp.where(row == s, slot_live, 0)
            ids = jnp.where(lane < row_live, slot_id, ids)
        meta_tx[g] = ids

    pl.semaphore_wait(barrier, 1 + (pairs - 1) + (groups - 1))
    for step in range(1, groups):
        target = lax.rem(me_dp + step, groups)
        send(
            meta_tx.at[target],
            meta_rx.at[groups - step],
            (meta_sem.at[0, step], meta_sem.at[1, groups - step]),
            {"dp": target},
        )
    meta_rx[0] = meta_tx[me_dp]

    loads[0].wait()
    normalise(res_v, enc_gain, normed, BLOCK)
    for index, (weight, target) in enumerate(((w_eq, e_q), (w_ek, e_k), (w_ev, e_v))):
        loads[1 + index].wait()
        project(normed, weight, target)

    block_lane = lax.broadcasted_iota(jnp.int32, (BLOCK, BLOCK), 1)

    def second_stage(r):
        arrive(rx1.at[r], (rs1_sem.at[0, r], rs1_sem.at[1, r]), {"tensor": partner})
        for step in range(1, pairs):
            target = lax.rem(pair + step, pairs)
            tx2[r, step - 1] = (
                part[r, side, target].astype(F32) + rx1[r, target].astype(F32)
            ).astype(BF16)
            send(
                tx2.at[r, step - 1],
                rx2.at[r, step - 1],
                (rs2_sem.at[0, r, step - 1], rs2_sem.at[1, r, step - 1]),
                {"tensor": peer(step)},
            )

    for r in range(2):
        first, last = r * half_blocks, (r + 1) * half_blocks
        key_first, key_last = max(first - 1, 0), min(last + 1, blocks)
        for b in range(first, last):
            for kb in range(key_first, key_last):
                seen = jnp.where(owner[b] == owner[kb], live[kb], 0)
                e_bias[
                    r,
                    (b - first) * BLOCK : (b - first + 1) * BLOCK,
                    (kb - key_first) * BLOCK : (kb - key_first + 1) * BLOCK,
                ] = jnp.where(block_lane < seen, 0.0, RAW_MASKED)
        key_count = (key_last - key_first) * BLOCK
        attend(
            e_q,
            e_k,
            e_v,
            e_bias.at[r, :, pl.ds(0, key_count)],
            e_ctx,
            pl.ds(r * half, half),
            pl.ds(key_first * BLOCK, key_count),
            heads,
        )
        if r == 0:
            loads[4].wait()
        tile = max(256, share)
        per_tile = tile // share
        for index in range(width // tile):
            sums = jnp.dot(
                e_ctx[r * half : (r + 1) * half, :],
                w_eo[:, index * tile : (index + 1) * tile],
                preferred_element_type=F32,
            )
            for inner in range(per_tile):
                j = index * per_tile + inner
                part[r, j % 2, j // 2] = sums[:, inner * share : (inner + 1) * share].astype(
                    BF16
                )
        send(
            part.at[r, 1 - side],
            rx1.at[r],
            (rs1_sem.at[0, r], rs1_sem.at[1, r]),
            {"tensor": partner},
        )
        if r == 0:
            loads[5].wait()
            normalise(dec_v, dec_gain, d_normed, BLOCK)
            second_stage(0)
    loads[6].wait()
    project(d_normed, w_cq, c_q)
    second_stage(1)

    for step in range(1, groups):
        arrive(
            meta_rx.at[step],
            (meta_sem.at[0, step], meta_sem.at[1, step]),
            {"dp": me_dp},
        )
    for q in range(query_rows // LANES):
        wanted = jnp.broadcast_to(
            query_protein[q : q + 1, :].astype(F32), (LANES, LANES)
        ).T
        for g in range(groups):
            for s in range(slots):
                named = meta_rx[g, s : s + 1, :].astype(F32)
                start = (g * slots + s) * BLOCK
                c_bias[q * LANES : (q + 1) * LANES, start : start + BLOCK] = jnp.where(
                    wanted == named, 0.0, RAW_MASKED
                )

    for r in range(2):
        rows = slice(r * half, (r + 1) * half)
        if share % LANES == 0:
            own = res_v[rows, pl.ds(pl.multiple_of(me_t * share, LANES), share)].astype(F32)
        else:
            own = jnp.zeros((half, share), F32)
            for j in range(tensors):
                mine = jnp.where(me_t == j, 1.0, 0.0)
                own = own + mine * res_v[rows, j * share : (j + 1) * share].astype(F32)
        sums = part[r, side, pair].astype(F32) + rx1[r, pair].astype(F32)
        for step in range(1, pairs):
            arrive(
                rx2.at[r, step - 1],
                (rs2_sem.at[0, r, step - 1], rs2_sem.at[1, r, step - 1]),
                {"tensor": partner},
            )
            sums = sums + rx2[r, step - 1].astype(F32)
        encoded[rows, :] = (own + sums).astype(BF16)

    for g in range(groups):
        for s in range(slots):
            block = jnp.zeros((BLOCK, share), F32)
            for b in range(blocks):
                match = (dest[b] == g) & (rank[b] == s)
                chosen = jnp.where(match, 1.0, 0.0)
                block = block + chosen * encoded[b * BLOCK : (b + 1) * BLOCK, :].astype(F32)
            placed[g, s * BLOCK : (s + 1) * BLOCK, :] = block.astype(BF16)
    for step in range(1, groups):
        target = lax.rem(me_dp + step, groups)
        send(
            placed.at[target],
            gath.at[groups - step, me_t],
            (a2a_sem.at[0, step], a2a_sem.at[1, groups - step]),
            {"dp": target},
        )
    gath[0, me_t] = placed[me_dp]

    def begin(g):
        if g > 0:
            arrive(
                gath.at[g, me_t], (a2a_sem.at[0, g], a2a_sem.at[1, g]), {"dp": me_dp}
            )
        for step in range(1, pairs):
            send(
                gath.at[g, me_t],
                gath.at[g, me_t],
                (ag_sem.at[0, g, step], ag_sem.at[1, g, step]),
                {"tensor": peer(step)},
            )
        send(
            gath.at[g, me_t],
            gath.at[g, me_t],
            (agp_sem.at[0, g, 0], agp_sem.at[1, g, 0]),
            {"tensor": partner},
        )

    def forward(g):
        for step in range(1, pairs):
            origin = lax.rem(pair + pairs - step, pairs) * 2 + side
            arrive(
                gath.at[g, origin],
                (ag_sem.at[0, g, step], ag_sem.at[1, g, step]),
                {"tensor": partner},
            )
            send(
                gath.at[g, origin],
                gath.at[g, origin],
                (agp_sem.at[0, g, step], agp_sem.at[1, g, step]),
                {"tensor": partner},
            )

    slot_rows = slots * BLOCK

    def keys_values(g):
        for step in range(pairs):
            origin = lax.rem(pair + pairs - step, pairs) * 2 + (1 - side)
            arrive(
                gath.at[g, origin],
                (agp_sem.at[0, g, step], agp_sem.at[1, g, step]),
                {"tensor": partner},
            )
        squares = jnp.zeros((slot_rows, 1), F32)
        for j in range(tensors):
            values = gath[g, j].astype(F32)
            squares = squares + jnp.sum(values * values, axis=1, keepdims=True)
            scaled[:, j * share : (j + 1) * share] = (
                values * final_gain[:, j * share : (j + 1) * share]
            ).astype(BF16)
        key_scale = lax.rsqrt(squares / width + EPSILON)
        rows = pl.ds(g * slot_rows, slot_rows)
        for weight, target in ((w_ck, c_k), (w_cv, c_v)):

            @pl.loop(0, weight.shape[1] // 256)
            def _(index):
                columns = pl.ds(pl.multiple_of(index * 256, 256), 256)
                sums = jnp.dot(scaled[...], weight[:, columns], preferred_element_type=F32)
                target[rows, columns] = (sums * key_scale).astype(BF16)

    loads[7].wait()
    loads[8].wait()
    begin(0)
    for g in range(1, groups + 2):
        if g < groups:
            begin(g)
        if g - 1 < groups:
            forward(g - 1)
        if g >= 2:
            keys_values(g - 2)

    attend(
        c_q,
        c_k,
        c_v,
        c_bias,
        c_ctx,
        pl.ds(0, query_rows),
        pl.ds(0, groups * slot_rows),
        heads,
        2 if groups * slot_rows <= 1024 else 1,
    )

    loads[9].wait()
    half_width = width // 2

    def decoder_stage(r):
        arrive(drx1.at[r], (drs1_sem.at[0, r], drs1_sem.at[1, r]), {"tensor": partner})
        for step in range(1, pairs):
            target = lax.rem(pair + step, pairs)
            dtx2[r, step - 1] = (
                dpart[r, side, target].astype(F32) + drx1[r, target].astype(F32)
            ).astype(BF16)
            send(
                dtx2.at[r, step - 1],
                drx2.at[r, step - 1],
                (drs2_sem.at[0, r, step - 1], drs2_sem.at[1, r, step - 1]),
                {"tensor": peer(step)},
            )

    for r in range(2):
        for index in range(half_width // 256):
            start = r * half_width + index * 256
            sums = jnp.dot(
                c_ctx[...], w_co[:, start : start + 256], preferred_element_type=F32
            )
            for j in range(tensors):
                piece = sums[j * row_share : (j + 1) * row_share, :]
                if row_pad > row_share:
                    piece = jnp.concatenate(
                        [piece, jnp.zeros((row_pad - row_share, 256), F32)], axis=0
                    )
                dpart[r, j % 2, j // 2, :, index * 256 : (index + 1) * 256] = piece.astype(
                    BF16
                )
        send(
            dpart.at[r, 1 - side],
            drx1.at[r],
            (drs1_sem.at[0, r], drs1_sem.at[1, r]),
            {"tensor": partner},
        )
    decoder_stage(0)
    decoder_stage(1)
    for r in range(2):
        columns = slice(r * half_width, (r + 1) * half_width)
        if row_share % 16 == 0:
            own = dec_v[pl.ds(pl.multiple_of(me_t * row_share, 16), row_share), columns]
            own = own.astype(F32)
        else:
            own = jnp.zeros((row_share, half_width), F32)
            everything = dec_v[:, columns].astype(F32)
            for j in range(tensors):
                mine = jnp.where(me_t == j, 1.0, 0.0)
                own = own + mine * everything[j * row_share : (j + 1) * row_share, :]
        sums = dpart[r, side, pair].astype(F32) + drx1[r, pair].astype(F32)
        for step in range(1, pairs):
            arrive(
                drx2.at[r, step - 1],
                (drs2_sem.at[0, r, step - 1], drs2_sem.at[1, r, step - 1]),
                {"tensor": partner},
            )
            sums = sums + drx2[r, step - 1].astype(F32)
        decoded[:, columns] = (own + sums[:row_share, :]).astype(BF16)

    for copy in sent:
        copy.wait_send()


def body(groups, tensors, *args):
    (
        residues,
        block_protein,
        protein_length,
        decoder_group,
        enc_gain,
        enc_query,
        enc_key,
        enc_value,
        enc_out,
        decoder_states,
        query_protein,
        dec_gain,
        final_gain,
        cross_query,
        cross_key,
        cross_value,
        cross_out,
    ) = args
    tok_rows, width = residues.shape
    query_rows = decoder_states.shape[0]
    inner = enc_query.shape[1]
    blocks = tok_rows // BLOCK
    slots = blocks // 2
    slot_rows = slots * BLOCK
    pairs = tensors // 2
    half = tok_rows // 2
    share = width // tensors
    row_share = query_rows // tensors
    row_pad = -(-row_share // 16) * 16
    keys = groups * slot_rows
    key_span = min(blocks, blocks // 2 + 1) * BLOCK
    hbm = pl.BlockSpec(memory_space=pl.ANY)
    smem = pl.BlockSpec(memory_space=pltpu.SMEM)
    vmem = pl.BlockSpec(memory_space=pltpu.VMEM)
    weight = pltpu.VMEM((width, inner), BF16)
    out_weight = pltpu.VMEM((inner, width), BF16)
    dma = pltpu.SemaphoreType.DMA
    return pl.pallas_call(
        functools.partial(kernel, groups, tensors),
        out_shape=(
            jax.ShapeDtypeStruct((tok_rows, share), BF16),
            jax.ShapeDtypeStruct((row_share, width), BF16),
        ),
        in_specs=[
            hbm,
            smem,
            smem,
            smem,
            vmem,
            hbm,
            hbm,
            hbm,
            hbm,
            hbm,
            vmem,
            vmem,
            vmem,
            hbm,
            hbm,
            hbm,
            hbm,
        ],
        out_specs=(vmem, vmem),
        scratch_shapes=[
            pltpu.VMEM((tok_rows, width), BF16),
            pltpu.VMEM((query_rows, width), BF16),
            weight,
            weight,
            weight,
            out_weight,
            weight,
            weight,
            weight,
            out_weight,
            pltpu.VMEM((tok_rows, width), BF16),
            pltpu.VMEM((tok_rows, inner), BF16),
            pltpu.VMEM((tok_rows, inner), BF16),
            pltpu.VMEM((tok_rows, inner), BF16),
            pltpu.VMEM((tok_rows, inner), BF16),
            pltpu.VMEM((2, half, key_span), F32),
            pltpu.VMEM((2, 2, pairs, half, share), BF16),
            pltpu.VMEM((2, pairs, half, share), BF16),
            pltpu.VMEM((2, pairs - 1, half, share), BF16),
            pltpu.VMEM((2, pairs - 1, half, share), BF16),
            pltpu.VMEM((groups, slot_rows, share), BF16),
            pltpu.VMEM((groups, tensors, slot_rows, share), BF16),
            pltpu.VMEM((groups, 8, LANES), jnp.int32),
            pltpu.VMEM((groups, 8, LANES), jnp.int32),
            pltpu.VMEM((query_rows, width), BF16),
            pltpu.VMEM((query_rows, inner), BF16),
            pltpu.VMEM((keys, inner), BF16),
            pltpu.VMEM((keys, inner), BF16),
            pltpu.VMEM((query_rows, inner), BF16),
            pltpu.VMEM((query_rows, keys), F32),
            pltpu.VMEM((slot_rows, width), BF16),
            pltpu.VMEM((2, 2, pairs, row_pad, width // 2), BF16),
            pltpu.VMEM((2, pairs, row_pad, width // 2), BF16),
            pltpu.VMEM((2, pairs - 1, row_pad, width // 2), BF16),
            pltpu.VMEM((2, pairs - 1, row_pad, width // 2), BF16),
            dma((10,)),
            dma((2, groups)),
            dma((2, 2)),
            dma((2, 2, pairs - 1)),
            dma((2, groups)),
            dma((2, groups, pairs)),
            dma((2, groups, pairs)),
            dma((2, 2)),
            dma((2, 2, pairs - 1)),
        ],
        compiler_params=pltpu.CompilerParams(
            collective_id=0,
            has_side_effects=True,
            vmem_limit_bytes=60 * 1024 * 1024,
        ),
    )(
        residues,
        block_protein,
        protein_length,
        decoder_group,
        enc_gain.reshape(1, width),
        enc_query,
        enc_key,
        enc_value,
        enc_out,
        decoder_states,
        query_protein.reshape(query_rows // LANES, LANES),
        dec_gain.reshape(1, width),
        final_gain.reshape(1, width),
        cross_query,
        cross_key,
        cross_value,
        cross_out,
    )


def solution(mesh):
    in_specs = (
        P("dp", None),
        P("dp"),
        P(),
        P(),
        P(),
        P(None, "tensor"),
        P(None, "tensor"),
        P(None, "tensor"),
        P("tensor", None),
        P("dp", None),
        P("dp"),
        P(),
        P(),
        P(None, "tensor"),
        P(None, "tensor"),
        P(None, "tensor"),
        P("tensor", None),
    )
    out_specs = (P("dp", "tensor"), P(("dp", "tensor"), None))
    return jax.shard_map(
        functools.partial(body, mesh.shape["dp"], mesh.shape["tensor"]),
        mesh=mesh,
        in_specs=in_specs,
        out_specs=out_specs,
        check_vma=False,
    )
```

```python
import functools

import jax
import jax.numpy as jnp
from jax import lax
from jax.experimental import pallas as pl
from jax.experimental.pallas import tpu as pltpu
from jax.sharding import PartitionSpec as P

HEAD_DIM = 128
BLOCK = 128
LANES = 128

EPSILON = 1e-06
LOG2E = 1.4426950408889634
MASKED = -1000000000.0
SCORE_SCALE = HEAD_DIM ** (-0.5)
QUERY_SCALE = SCORE_SCALE * LOG2E
RAW_MASKED = MASKED * LOG2E
MESH = pl.DeviceIdType.MESH
F32 = jnp.float32
BF16 = jnp.bfloat16


def normalise(source, gain, target, rows):
    for start in range(0, source.shape[0], rows):
        values = source[start : start + rows, :].astype(F32)
        scale = lax.rsqrt(jnp.mean(values * values, axis=1, keepdims=True) + EPSILON)
        target[start : start + rows, :] = (values * scale * gain[...]).astype(BF16)


def project(source, weight, target, scale=None, tile=512):
    @pl.loop(0, weight.shape[1] // tile)
    def _(index):
        columns = pl.ds(pl.multiple_of(index * tile, tile), tile)
        sums = jnp.dot(source[...], weight[:, columns], preferred_element_type=F32)
        if scale is not None:
            sums = sums * scale
        target[:, columns] = sums.astype(BF16)


def project_values(source, weight, target, scale=None, tile=512):
    @pl.loop(0, weight.shape[1] // tile)
    def _(index):
        columns = pl.ds(pl.multiple_of(index * tile, tile), tile)
        sums = jnp.dot(source[...], weight[:, columns], preferred_element_type=F32)
        if scale is not None:
            sums = sums * scale
        for head in range(tile // HEAD_DIM):
            start = pl.multiple_of(index * 2 * tile + head * 2 * HEAD_DIM, 2 * HEAD_DIM)
            target[:, pl.ds(start, HEAD_DIM)] = sums[
                :, head * HEAD_DIM : (head + 1) * HEAD_DIM
            ].astype(BF16)


def fill_ones(target):
    ones = jnp.ones((target.shape[0], HEAD_DIM), BF16)
    for start in range(HEAD_DIM, target.shape[1], 2 * HEAD_DIM):
        target[:, start : start + HEAD_DIM] = ones


def raw_scores(queries, keys):
    return lax.dot_general(
        queries, keys, (((1,), (1,)), ((), ())), preferred_element_type=F32
    )


def attend(queries, keys, values, bias, context, q_rows, k_rows, heads, together=2):
    @pl.loop(0, heads // together)
    def _(index):
        for inner in range(together):
            head = index * together + inner
            columns = pl.ds(pl.multiple_of(head * HEAD_DIM, HEAD_DIM), HEAD_DIM)
            both = pl.ds(pl.multiple_of(head * 2 * HEAD_DIM, HEAD_DIM), 2 * HEAD_DIM)
            scores = raw_scores(queries[q_rows, columns], keys[k_rows, columns]) + bias[...]
            expo = jnp.exp2(scores - jnp.max(scores, axis=1, keepdims=True))
            mixed = jnp.dot(
                expo.astype(BF16), values[k_rows, both], preferred_element_type=F32
            )
            context[q_rows, columns] = (mixed[:, :HEAD_DIM] / mixed[:, HEAD_DIM:]).astype(BF16)


def attend_part(queries, keys, values, bias, tops, sums, context, heads, first, last, together=2):
    spread = keys.shape[0] // HEAD_DIM

    @pl.loop(0, heads // together)
    def _(index):
        for inner in range(together):
            head = index * together + inner
            columns = pl.ds(pl.multiple_of(head * HEAD_DIM, HEAD_DIM), HEAD_DIM)
            both = pl.ds(pl.multiple_of(head * 2 * HEAD_DIM, HEAD_DIM), 2 * HEAD_DIM)
            scores = raw_scores(queries[:, columns], keys[:, columns]) + bias[...]
            top = jnp.broadcast_to(
                jnp.max(scores, axis=1, keepdims=True), (scores.shape[0], HEAD_DIM)
            )
            if not first:
                before = tops[head]
                top = jnp.maximum(top, before)
            expo = jnp.exp2(scores - jnp.concatenate([top] * spread, axis=1))
            mixed = jnp.dot(expo.astype(BF16), values[:, both], preferred_element_type=F32)
            if not first:
                decay = jnp.exp2(before - top)
                mixed = mixed + sums[head] * jnp.concatenate([decay] * 2, axis=1)
            if last:
                context[:, columns] = (mixed[:, :HEAD_DIM] / mixed[:, HEAD_DIM:]).astype(BF16)
            else:
                tops[head] = top
                sums[head] = mixed


def kernel(
    groups,
    tensors,
    residues,
    block_protein,
    protein_length,
    decoder_group,
    enc_gain,
    enc_query,
    enc_key,
    enc_value,
    enc_out,
    decoder_states,
    query_protein,
    dec_gain,
    final_gain,
    cross_query,
    cross_key,
    cross_value,
    cross_out,
    encoded,
    decoded,
    res_v,
    dec_v,
    w_eq,
    w_ek,
    w_ev,
    w_eo,
    w_cq,
    w_ck,
    w_cv,
    w_co,
    normed,
    e_q,
    e_k,
    e_v,
    e_ctx,
    e_bias,
    part,
    rx1,
    tx2,
    rx2,
    placed,
    gath,
    meta_tx,
    meta_rx,
    d_normed,
    c_q,
    c_k,
    c_v,
    c_ctx,
    c_bias,
    c_tops,
    c_sums,
    scaled,
    dpart,
    drx1,
    dtx2,
    drx2,
    load_sem,
    meta_sem,
    rs1_sem,
    rs2_sem,
    a2a_sem,
    ag_sem,
    agp_sem,
    drs1_sem,
    drs2_sem,
):
    me_dp = lax.axis_index("dp")
    me_t = lax.axis_index("tensor")
    pairs = tensors // 2
    pair = me_t // 2
    side = lax.rem(me_t, 2)
    partner = pair * 2 + (1 - side)
    tok_rows, width = res_v.shape
    blocks = tok_rows // BLOCK
    slots = blocks // 2
    heads = e_q.shape[1] // HEAD_DIM
    half = tok_rows // 2
    half_blocks = blocks // 2
    share = encoded.shape[1]
    query_rows = dec_v.shape[0]
    row_share = query_rows // tensors
    row_pad = dpart.shape[3]

    def peer(step):
        return lax.rem(pair + step, pairs) * 2 + side

    loads = []
    for index, (src, dst) in enumerate(
        (
            (residues, res_v),
            (enc_query, w_eq),
            (enc_key, w_ek),
            (enc_value, w_ev),
            (enc_out, w_eo),
            (decoder_states, dec_v),
            (cross_query, w_cq),
            (cross_key, w_ck),
            (cross_value, w_cv),
            (cross_out, w_co),
        )
    ):
        load = pltpu.make_async_copy(src, dst, load_sem.at[index])
        load.start()
        loads.append(load)

    barrier = pltpu.get_barrier_semaphore()
    pl.semaphore_signal(barrier, inc=1, device_id={"tensor": partner}, device_id_type=MESH)
    for step in range(1, pairs):
        pl.semaphore_signal(
            barrier, inc=1, device_id={"tensor": peer(step)}, device_id_type=MESH
        )
    for step in range(1, groups):
        pl.semaphore_signal(
            barrier,
            inc=1,
            device_id={"dp": lax.rem(me_dp + step, groups)},
            device_id_type=MESH,
        )

    sent = []

    def send(src, dst, sems, device):
        copy = pltpu.make_async_remote_copy(
            src_ref=src,
            dst_ref=dst,
            send_sem=sems[0],
            recv_sem=sems[1],
            device_id=device,
            device_id_type=MESH,
        )
        copy.start()
        sent.append(copy)

    def arrive(dst, sems, device):
        pltpu.make_async_remote_copy(
            src_ref=dst,
            dst_ref=dst,
            send_sem=sems[0],
            recv_sem=sems[1],
            device_id=device,
            device_id_type=MESH,
        ).wait_recv()

    owner = [block_protein[b] for b in range(blocks)]
    live, dest, rank = [], [], []
    for b in range(blocks):
        offset = jnp.int32(0)
        for other in range(b):
            offset = offset + jnp.where(owner[other] == owner[b], 1, 0)
        length = protein_length[owner[b]]
        live.append(jnp.clip(length - offset * BLOCK, 0, BLOCK))
        dest.append(decoder_group[owner[b]])
    for b in range(blocks):
        place = jnp.int32(0)
        for other in range(b):
            place = place + jnp.where(dest[other] == dest[b], 1, 0)
        rank.append(place)

    lane = lax.broadcasted_iota(jnp.int32, (8, LANES), 1)
    row = lax.broadcasted_iota(jnp.int32, (8, LANES), 0)
    for g in range(groups):
        ids = jnp.full((8, LANES), -1, jnp.int32)
        for s in range(slots):
            slot_id, slot_live = jnp.int32(-1), jnp.int32(0)
            for b in range(blocks):
                match = (dest[b] == g) & (rank[b] == s)
                slot_id = jnp.where(match, owner[b], slot_id)
                slot_live = jnp.where(match, live[b], slot_live)
            row_live = jnp.where(row == s, slot_live, 0)
            ids = jnp.where(lane < row_live, slot_id, ids)
        meta_tx[g] = ids

    pl.semaphore_wait(barrier, 1 + (pairs - 1) + (groups - 1))
    for step in range(1, groups):
        target = lax.rem(me_dp + step, groups)
        send(
            meta_tx.at[target],
            meta_rx.at[groups - step],
            (meta_sem.at[0, step], meta_sem.at[1, groups - step]),
            {"dp": target},
        )
    meta_rx[0] = meta_tx[me_dp]

    loads[0].wait()
    normalise(res_v, enc_gain, normed, BLOCK)
    fill_ones(e_v)
    fill_ones(c_v)
    loads[1].wait()
    project(normed, w_eq, e_q, QUERY_SCALE)
    loads[2].wait()
    project(normed, w_ek, e_k)
    loads[3].wait()
    project_values(normed, w_ev, e_v)

    block_lane = lax.broadcasted_iota(jnp.int32, (BLOCK, BLOCK), 1)

    def second_stage(r):
        arrive(rx1.at[r], (rs1_sem.at[0, r], rs1_sem.at[1, r]), {"tensor": partner})
        for step in range(1, pairs):
            target = lax.rem(pair + step, pairs)
            tx2[r, step - 1] = (
                part[r, side, target].astype(F32) + rx1[r, target].astype(F32)
            ).astype(BF16)
            send(
                tx2.at[r, step - 1],
                rx2.at[r, step - 1],
                (rs2_sem.at[0, r, step - 1], rs2_sem.at[1, r, step - 1]),
                {"tensor": peer(step)},
            )

    for r in range(2):
        first, last = r * half_blocks, (r + 1) * half_blocks
        key_first, key_last = max(first - 1, 0), min(last + 1, blocks)
        for b in range(first, last):
            for kb in range(key_first, key_last):
                seen = jnp.where(owner[b] == owner[kb], live[kb], 0)
                e_bias[
                    r,
                    (b - first) * BLOCK : (b - first + 1) * BLOCK,
                    (kb - key_first) * BLOCK : (kb - key_first + 1) * BLOCK,
                ] = jnp.where(block_lane < seen, 0.0, RAW_MASKED)
        key_count = (key_last - key_first) * BLOCK
        attend(
            e_q,
            e_k,
            e_v,
            e_bias.at[r, :, pl.ds(0, key_count)],
            e_ctx,
            pl.ds(r * half, half),
            pl.ds(key_first * BLOCK, key_count),
            heads,
        )
        if r == 0:
            loads[4].wait()
        tile = max(256, share)
        per_tile = tile // share
        for index in range(width // tile):
            sums = jnp.dot(
                e_ctx[r * half : (r + 1) * half, :],
                w_eo[:, index * tile : (index + 1) * tile],
                preferred_element_type=F32,
            )
            for inner in range(per_tile):
                j = index * per_tile + inner
                part[r, j % 2, j // 2] = sums[:, inner * share : (inner + 1) * share].astype(
                    BF16
                )
        send(
            part.at[r, 1 - side],
            rx1.at[r],
            (rs1_sem.at[0, r], rs1_sem.at[1, r]),
            {"tensor": partner},
        )
        if r == 0:
            loads[5].wait()
            normalise(dec_v, dec_gain, d_normed, BLOCK)
            second_stage(0)
    loads[6].wait()
    project(d_normed, w_cq, c_q, QUERY_SCALE)
    second_stage(1)

    for step in range(1, groups):
        arrive(
            meta_rx.at[step],
            (meta_sem.at[0, step], meta_sem.at[1, step]),
            {"dp": me_dp},
        )
    for q in range(query_rows // LANES):
        wanted = jnp.broadcast_to(
            query_protein[q : q + 1, :].astype(F32), (LANES, LANES)
        ).T
        for g in range(groups):
            for s in range(slots):
                named = meta_rx[g, s : s + 1, :].astype(F32)
                start = (g * slots + s) * BLOCK
                c_bias[q * LANES : (q + 1) * LANES, start : start + BLOCK] = jnp.where(
                    wanted == named, 0.0, RAW_MASKED
                )

    for r in range(2):
        rows = slice(r * half, (r + 1) * half)
        if share % LANES == 0:
            own = res_v[rows, pl.ds(pl.multiple_of(me_t * share, LANES), share)].astype(F32)
        else:
            own = jnp.zeros((half, share), F32)
            for j in range(tensors):
                mine = jnp.where(me_t == j, 1.0, 0.0)
                own = own + mine * res_v[rows, j * share : (j + 1) * share].astype(F32)
        sums = part[r, side, pair].astype(F32) + rx1[r, pair].astype(F32)
        for step in range(1, pairs):
            arrive(
                rx2.at[r, step - 1],
                (rs2_sem.at[0, r, step - 1], rs2_sem.at[1, r, step - 1]),
                {"tensor": partner},
            )
            sums = sums + rx2[r, step - 1].astype(F32)
        encoded[rows, :] = (own + sums).astype(BF16)

    for g in range(groups):
        for s in range(slots):
            block = jnp.zeros((BLOCK, share), F32)
            for b in range(blocks):
                match = (dest[b] == g) & (rank[b] == s)
                chosen = jnp.where(match, 1.0, 0.0)
                block = block + chosen * encoded[b * BLOCK : (b + 1) * BLOCK, :].astype(F32)
            placed[g, s * BLOCK : (s + 1) * BLOCK, :] = block.astype(BF16)
    for step in range(1, groups):
        target = lax.rem(me_dp + step, groups)
        send(
            placed.at[target],
            gath.at[groups - step, me_t],
            (a2a_sem.at[0, step], a2a_sem.at[1, groups - step]),
            {"dp": target},
        )
    gath[0, me_t] = placed[me_dp]

    def begin(g):
        if g > 0:
            arrive(
                gath.at[g, me_t], (a2a_sem.at[0, g], a2a_sem.at[1, g]), {"dp": me_dp}
            )
        for step in range(1, pairs):
            send(
                gath.at[g, me_t],
                gath.at[g, me_t],
                (ag_sem.at[0, g, step], ag_sem.at[1, g, step]),
                {"tensor": peer(step)},
            )
        send(
            gath.at[g, me_t],
            gath.at[g, me_t],
            (agp_sem.at[0, g, 0], agp_sem.at[1, g, 0]),
            {"tensor": partner},
        )

    def forward(g):
        for step in range(1, pairs):
            origin = lax.rem(pair + pairs - step, pairs) * 2 + side
            arrive(
                gath.at[g, origin],
                (ag_sem.at[0, g, step], ag_sem.at[1, g, step]),
                {"tensor": partner},
            )
            send(
                gath.at[g, origin],
                gath.at[g, origin],
                (agp_sem.at[0, g, step], agp_sem.at[1, g, step]),
                {"tensor": partner},
            )

    slot_rows = slots * BLOCK

    def keys_values(g):
        for step in range(pairs):
            origin = lax.rem(pair + pairs - step, pairs) * 2 + (1 - side)
            arrive(
                gath.at[g, origin],
                (agp_sem.at[0, g, step], agp_sem.at[1, g, step]),
                {"tensor": partner},
            )
        squares = jnp.zeros((slot_rows, 1), F32)
        for j in range(tensors):
            values = gath[g, j].astype(F32)
            squares = squares + jnp.sum(values * values, axis=1, keepdims=True)
            scaled[:, j * share : (j + 1) * share] = (
                values * final_gain[:, j * share : (j + 1) * share]
            ).astype(BF16)
        key_scale = lax.rsqrt(squares / width + EPSILON)
        project(scaled, w_ck, c_k, key_scale)
        project_values(scaled, w_cv, c_v, key_scale)
        attend_part(
            c_q,
            c_k,
            c_v,
            c_bias.at[:, pl.ds(g * slot_rows, slot_rows)],
            c_tops,
            c_sums,
            c_ctx,
            heads,
            g == 0,
            g == groups - 1,
        )

    loads[7].wait()
    loads[8].wait()
    begin(0)
    for g in range(1, groups + 2):
        if g < groups:
            begin(g)
        if g - 1 < groups:
            forward(g - 1)
        if g >= 2:
            keys_values(g - 2)

    loads[9].wait()
    half_width = width // 2

    def decoder_stage(r):
        arrive(drx1.at[r], (drs1_sem.at[0, r], drs1_sem.at[1, r]), {"tensor": partner})
        for step in range(1, pairs):
            target = lax.rem(pair + step, pairs)
            dtx2[r, step - 1] = (
                dpart[r, side, target].astype(F32) + drx1[r, target].astype(F32)
            ).astype(BF16)
            send(
                dtx2.at[r, step - 1],
                drx2.at[r, step - 1],
                (drs2_sem.at[0, r, step - 1], drs2_sem.at[1, r, step - 1]),
                {"tensor": peer(step)},
            )

    for r in range(2):
        for index in range(half_width // 256):
            start = r * half_width + index * 256
            sums = jnp.dot(
                c_ctx[...], w_co[:, start : start + 256], preferred_element_type=F32
            )
            for j in range(tensors):
                piece = sums[j * row_share : (j + 1) * row_share, :]
                if row_pad > row_share:
                    piece = jnp.concatenate(
                        [piece, jnp.zeros((row_pad - row_share, 256), F32)], axis=0
                    )
                dpart[r, j % 2, j // 2, :, index * 256 : (index + 1) * 256] = piece.astype(
                    BF16
                )
        send(
            dpart.at[r, 1 - side],
            drx1.at[r],
            (drs1_sem.at[0, r], drs1_sem.at[1, r]),
            {"tensor": partner},
        )
    decoder_stage(0)
    decoder_stage(1)
    for r in range(2):
        columns = slice(r * half_width, (r + 1) * half_width)
        if row_share % 16 == 0:
            own = dec_v[pl.ds(pl.multiple_of(me_t * row_share, 16), row_share), columns]
            own = own.astype(F32)
        else:
            own = jnp.zeros((row_share, half_width), F32)
            everything = dec_v[:, columns].astype(F32)
            for j in range(tensors):
                mine = jnp.where(me_t == j, 1.0, 0.0)
                own = own + mine * everything[j * row_share : (j + 1) * row_share, :]
        sums = dpart[r, side, pair].astype(F32) + drx1[r, pair].astype(F32)
        for step in range(1, pairs):
            arrive(
                drx2.at[r, step - 1],
                (drs2_sem.at[0, r, step - 1], drs2_sem.at[1, r, step - 1]),
                {"tensor": partner},
            )
            sums = sums + drx2[r, step - 1].astype(F32)
        decoded[:, columns] = (own + sums[:row_share, :]).astype(BF16)

    for copy in sent:
        copy.wait_send()


def hand_over(first, second, first_out, second_out, sems):
    copies = [
        pltpu.make_async_copy(first, first_out, sems.at[0]),
        pltpu.make_async_copy(second, second_out, sems.at[1]),
    ]
    for copy in copies:
        copy.start()
    for copy in copies:
        copy.wait()


def body(groups, tensors, *args):
    (
        residues,
        block_protein,
        protein_length,
        decoder_group,
        enc_gain,
        enc_query,
        enc_key,
        enc_value,
        enc_out,
        decoder_states,
        query_protein,
        dec_gain,
        final_gain,
        cross_query,
        cross_key,
        cross_value,
        cross_out,
    ) = args
    tok_rows, width = residues.shape
    query_rows = decoder_states.shape[0]
    inner = enc_query.shape[1]
    blocks = tok_rows // BLOCK
    slots = blocks // 2
    slot_rows = slots * BLOCK
    pairs = tensors // 2
    half = tok_rows // 2
    share = width // tensors
    row_share = query_rows // tensors
    row_pad = -(-row_share // 16) * 16
    keys = groups * slot_rows
    key_span = min(blocks, blocks // 2 + 1) * BLOCK
    hbm = pl.BlockSpec(memory_space=pl.ANY)
    smem = pl.BlockSpec(memory_space=pltpu.SMEM)
    vmem = pl.BlockSpec(memory_space=pltpu.VMEM)
    weight = pltpu.VMEM((width, inner), BF16)
    out_weight = pltpu.VMEM((inner, width), BF16)
    dma = pltpu.SemaphoreType.DMA
    results = pl.pallas_call(
        functools.partial(kernel, groups, tensors),
        out_shape=(
            jax.ShapeDtypeStruct((tok_rows, share), BF16),
            jax.ShapeDtypeStruct((row_share, width), BF16),
        ),
        in_specs=[
            hbm,
            smem,
            smem,
            smem,
            vmem,
            hbm,
            hbm,
            hbm,
            hbm,
            hbm,
            vmem,
            vmem,
            vmem,
            hbm,
            hbm,
            hbm,
            hbm,
        ],
        out_specs=(vmem, vmem),
        scratch_shapes=[
            pltpu.VMEM((tok_rows, width), BF16),
            pltpu.VMEM((query_rows, width), BF16),
            weight,
            weight,
            weight,
            out_weight,
            weight,
            weight,
            weight,
            out_weight,
            pltpu.VMEM((tok_rows, width), BF16),
            pltpu.VMEM((tok_rows, inner), BF16),
            pltpu.VMEM((tok_rows, inner), BF16),
            pltpu.VMEM((tok_rows, 2 * inner), BF16),
            pltpu.VMEM((tok_rows, inner), BF16),
            pltpu.VMEM((2, half, key_span), F32),
            pltpu.VMEM((2, 2, pairs, half, share), BF16),
            pltpu.VMEM((2, pairs, half, share), BF16),
            pltpu.VMEM((2, pairs - 1, half, share), BF16),
            pltpu.VMEM((2, pairs - 1, half, share), BF16),
            pltpu.VMEM((groups, slot_rows, share), BF16),
            pltpu.VMEM((groups, tensors, slot_rows, share), BF16),
            pltpu.VMEM((groups, 8, LANES), jnp.int32),
            pltpu.VMEM((groups, 8, LANES), jnp.int32),
            pltpu.VMEM((query_rows, width), BF16),
            pltpu.VMEM((query_rows, inner), BF16),
            pltpu.VMEM((slot_rows, inner), BF16),
            pltpu.VMEM((slot_rows, 2 * inner), BF16),
            pltpu.VMEM((query_rows, inner), BF16),
            pltpu.VMEM((query_rows, keys), F32),
            pltpu.VMEM((inner // HEAD_DIM, query_rows, HEAD_DIM), F32),
            pltpu.VMEM((inner // HEAD_DIM, query_rows, 2 * HEAD_DIM), F32),
            pltpu.VMEM((slot_rows, width), BF16),
            pltpu.VMEM((2, 2, pairs, row_pad, width // 2), BF16),
            pltpu.VMEM((2, pairs, row_pad, width // 2), BF16),
            pltpu.VMEM((2, pairs - 1, row_pad, width // 2), BF16),
            pltpu.VMEM((2, pairs - 1, row_pad, width // 2), BF16),
            dma((10,)),
            dma((2, groups)),
            dma((2, 2)),
            dma((2, 2, pairs - 1)),
            dma((2, groups)),
            dma((2, groups, pairs)),
            dma((2, groups, pairs)),
            dma((2, 2)),
            dma((2, 2, pairs - 1)),
        ],
        compiler_params=pltpu.CompilerParams(
            collective_id=0,
            has_side_effects=True,
            vmem_limit_bytes=60 * 1024 * 1024,
        ),
    )(
        residues,
        block_protein,
        protein_length,
        decoder_group,
        enc_gain.reshape(1, width),
        enc_query,
        enc_key,
        enc_value,
        enc_out,
        decoder_states,
        query_protein.reshape(query_rows // LANES, LANES),
        dec_gain.reshape(1, width),
        final_gain.reshape(1, width),
        cross_query,
        cross_key,
        cross_value,
        cross_out,
    )


    return pl.pallas_call(
        hand_over,
        out_shape=tuple(jax.ShapeDtypeStruct(r.shape, r.dtype) for r in results),
        in_specs=[hbm, hbm],
        out_specs=(hbm, hbm),
        scratch_shapes=[dma((2,))],
        compiler_params=pltpu.CompilerParams(vmem_limit_bytes=60 * 1024 * 1024),
    )(*results)


def solution(mesh):
    in_specs = (
        P("dp", None),
        P("dp"),
        P(),
        P(),
        P(),
        P(None, "tensor"),
        P(None, "tensor"),
        P(None, "tensor"),
        P("tensor", None),
        P("dp", None),
        P("dp"),
        P(),
        P(),
        P(None, "tensor"),
        P(None, "tensor"),
        P(None, "tensor"),
        P("tensor", None),
    )
    out_specs = (P("dp", "tensor"), P(("dp", "tensor"), None))
    return jax.shard_map(
        functools.partial(body, mesh.shape["dp"], mesh.shape["tensor"]),
        mesh=mesh,
        in_specs=in_specs,
        out_specs=out_specs,
        check_vma=False,
    )
```

```python
import functools

import jax
import jax.numpy as jnp
from jax import lax
from jax.experimental import pallas as pl
from jax.experimental.pallas import tpu as pltpu
from jax.sharding import PartitionSpec as P

HEAD_DIM = 128
BLOCK = 128
LANES = 128

EPSILON = 1e-06
LOG2E = 1.4426950408889634
MASKED = -1000000000.0
SCORE_SCALE = HEAD_DIM ** (-0.5)
QUERY_SCALE = SCORE_SCALE * LOG2E
RAW_MASKED = MASKED * LOG2E
MESH = pl.DeviceIdType.MESH
F32 = jnp.float32
BF16 = jnp.bfloat16


def normalise(source, gain, target, rows):
    for start in range(0, source.shape[0], rows):
        values = source[start : start + rows, :].astype(F32)
        scale = lax.rsqrt(jnp.mean(values * values, axis=1, keepdims=True) + EPSILON)
        target[start : start + rows, :] = (values * scale * gain[...]).astype(BF16)


def project(source, weight, target, scale=None, tile=512):
    for start in range(0, weight.shape[1], tile):
        columns = slice(start, start + tile)
        sums = jnp.dot(source[...], weight[:, columns], preferred_element_type=F32)
        if scale is not None:
            sums = sums * scale
        target[:, columns] = sums.astype(BF16)


def project_values(source, weight, target, scale=None, tile=512):
    for start in range(0, weight.shape[1], tile):
        sums = jnp.dot(
            source[...], weight[:, start : start + tile], preferred_element_type=F32
        )
        if scale is not None:
            sums = sums * scale
        for inner in range(0, tile, HEAD_DIM):
            place = 2 * (start + inner)
            target[:, place : place + HEAD_DIM] = sums[:, inner : inner + HEAD_DIM].astype(BF16)


def fill_ones(target):
    ones = jnp.ones((target.shape[0], HEAD_DIM), BF16)
    for start in range(HEAD_DIM, target.shape[1], 2 * HEAD_DIM):
        target[:, start : start + HEAD_DIM] = ones


def raw_scores(queries, keys):
    return lax.dot_general(
        queries, keys, (((1,), (1,)), ((), ())), preferred_element_type=F32
    )


def head_columns(group, together):
    single, double = [], []
    for inner in range(together):
        head = group * together + inner
        single.append(slice(head * HEAD_DIM, (head + 1) * HEAD_DIM))
        double.append(slice(2 * head * HEAD_DIM, 2 * (head + 1) * HEAD_DIM))
    return list(zip(single, double))


def attend(queries, keys, values, bias, context, q_rows, k_rows, heads, together=4):
    for group in range(heads // together):
        places = head_columns(group, together)
        scores = [
            raw_scores(queries[q_rows, one], keys[k_rows, one]) + bias[...] for one, _ in places
        ]
        weights = [
            jnp.exp2(one - jnp.max(one, axis=1, keepdims=True)).astype(BF16) for one in scores
        ]
        mixed = [
            jnp.dot(weight, values[k_rows, two], preferred_element_type=F32)
            for weight, (_, two) in zip(weights, places)
        ]
        for value, (one, _) in zip(mixed, places):
            context[q_rows, one] = (value[:, :HEAD_DIM] / value[:, HEAD_DIM:]).astype(BF16)


def attend_part(queries, keys, values, bias, tops, sums, context, heads, first, last, together=4):
    spread = keys.shape[0] // HEAD_DIM
    for group in range(heads // together):
        places = head_columns(group, together)
        base = group * together
        scores = [raw_scores(queries[:, one], keys[:, one]) + bias[...] for one, _ in places]
        highest = [
            jnp.broadcast_to(jnp.max(one, axis=1, keepdims=True), (one.shape[0], HEAD_DIM))
            for one in scores
        ]
        if not first:
            before = [tops[base + inner] for inner in range(together)]
            highest = [jnp.maximum(a, b) for a, b in zip(highest, before)]
        weights = [
            jnp.exp2(one - jnp.concatenate([top] * spread, axis=1)).astype(BF16)
            for one, top in zip(scores, highest)
        ]
        mixed = [
            jnp.dot(weight, values[:, two], preferred_element_type=F32)
            for weight, (_, two) in zip(weights, places)
        ]
        if not first:
            decays = [jnp.exp2(b - a) for a, b in zip(highest, before)]
            mixed = [
                value + sums[base + inner] * jnp.concatenate([decays[inner]] * 2, axis=1)
                for inner, value in enumerate(mixed)
            ]
        for inner, (one, _) in enumerate(places):
            value = mixed[inner]
            if last:
                context[:, one] = (value[:, :HEAD_DIM] / value[:, HEAD_DIM:]).astype(BF16)
            else:
                tops[base + inner] = highest[inner]
                sums[base + inner] = value


def kernel(
    groups,
    tensors,
    residues,
    block_protein,
    protein_length,
    decoder_group,
    enc_gain,
    enc_query,
    enc_key,
    enc_value,
    enc_out,
    decoder_states,
    query_protein,
    dec_gain,
    final_gain,
    cross_query,
    cross_key,
    cross_value,
    cross_out,
    encoded,
    decoded,
    res_v,
    dec_v,
    w_eq,
    w_ek,
    w_ev,
    w_eo,
    w_cq,
    w_ck,
    w_cv,
    w_co,
    normed,
    e_q,
    e_k,
    e_v,
    e_ctx,
    e_bias,
    part,
    rx1,
    tx2,
    rx2,
    placed,
    gath,
    meta_tx,
    meta_rx,
    d_normed,
    c_q,
    c_k,
    c_v,
    c_ctx,
    c_bias,
    c_tops,
    c_sums,
    scaled,
    dpart,
    drx1,
    dtx2,
    drx2,
    load_sem,
    meta_sem,
    rs1_sem,
    rs2_sem,
    a2a_sem,
    ag_sem,
    agp_sem,
    drs1_sem,
    drs2_sem,
):
    me_dp = lax.axis_index("dp")
    me_t = lax.axis_index("tensor")
    pairs = tensors // 2
    pair = me_t // 2
    side = lax.rem(me_t, 2)
    partner = pair * 2 + (1 - side)
    tok_rows, width = res_v.shape
    blocks = tok_rows // BLOCK
    slots = blocks // 2
    heads = e_q.shape[1] // HEAD_DIM
    half = tok_rows // 2
    half_blocks = blocks // 2
    share = encoded.shape[1]
    query_rows = dec_v.shape[0]
    row_share = query_rows // tensors
    row_pad = dpart.shape[3]

    def peer(step):
        return lax.rem(pair + step, pairs) * 2 + side

    loads = []
    for index, (src, dst) in enumerate(
        (
            (residues, res_v),
            (enc_query, w_eq),
            (enc_key, w_ek),
            (enc_value, w_ev),
            (enc_out, w_eo),
            (decoder_states, dec_v),
            (cross_query, w_cq),
            (cross_key, w_ck),
            (cross_value, w_cv),
            (cross_out, w_co),
        )
    ):
        load = pltpu.make_async_copy(src, dst, load_sem.at[index])
        load.start()
        loads.append(load)

    barrier = pltpu.get_barrier_semaphore()
    pl.semaphore_signal(barrier, inc=1, device_id={"tensor": partner}, device_id_type=MESH)
    for step in range(1, pairs):
        pl.semaphore_signal(
            barrier, inc=1, device_id={"tensor": peer(step)}, device_id_type=MESH
        )
    for step in range(1, groups):
        pl.semaphore_signal(
            barrier,
            inc=1,
            device_id={"dp": lax.rem(me_dp + step, groups)},
            device_id_type=MESH,
        )

    sent = []

    def send(src, dst, sems, device):
        copy = pltpu.make_async_remote_copy(
            src_ref=src,
            dst_ref=dst,
            send_sem=sems[0],
            recv_sem=sems[1],
            device_id=device,
            device_id_type=MESH,
        )
        copy.start()
        sent.append(copy)

    def arrive(dst, sems, device):
        pltpu.make_async_remote_copy(
            src_ref=dst,
            dst_ref=dst,
            send_sem=sems[0],
            recv_sem=sems[1],
            device_id=device,
            device_id_type=MESH,
        ).wait_recv()

    owner = [block_protein[b] for b in range(blocks)]
    live, dest, rank = [], [], []
    for b in range(blocks):
        offset = jnp.int32(0)
        for other in range(b):
            offset = offset + jnp.where(owner[other] == owner[b], 1, 0)
        length = protein_length[owner[b]]
        live.append(jnp.clip(length - offset * BLOCK, 0, BLOCK))
        dest.append(decoder_group[owner[b]])
    for b in range(blocks):
        place = jnp.int32(0)
        for other in range(b):
            place = place + jnp.where(dest[other] == dest[b], 1, 0)
        rank.append(place)

    lane = lax.broadcasted_iota(jnp.int32, (8, LANES), 1)
    row = lax.broadcasted_iota(jnp.int32, (8, LANES), 0)
    for g in range(groups):
        ids = jnp.full((8, LANES), -1, jnp.int32)
        for s in range(slots):
            slot_id, slot_live = jnp.int32(-1), jnp.int32(0)
            for b in range(blocks):
                match = (dest[b] == g) & (rank[b] == s)
                slot_id = jnp.where(match, owner[b], slot_id)
                slot_live = jnp.where(match, live[b], slot_live)
            row_live = jnp.where(row == s, slot_live, 0)
            ids = jnp.where(lane < row_live, slot_id, ids)
        meta_tx[g] = ids

    fill_ones(e_v)
    fill_ones(c_v)
    loads[0].wait()
    normalise(res_v, enc_gain, normed, BLOCK)
    loads[1].wait()
    project(normed, w_eq, e_q, QUERY_SCALE)
    loads[2].wait()
    project(normed, w_ek, e_k)
    loads[3].wait()
    project_values(normed, w_ev, e_v)

    pl.semaphore_wait(barrier, 1 + (pairs - 1) + (groups - 1))
    for step in range(1, groups):
        target = lax.rem(me_dp + step, groups)
        send(
            meta_tx.at[target],
            meta_rx.at[groups - step],
            (meta_sem.at[0, step], meta_sem.at[1, groups - step]),
            {"dp": target},
        )
    meta_rx[0] = meta_tx[me_dp]

    block_lane = lax.broadcasted_iota(jnp.int32, (BLOCK, BLOCK), 1)

    def second_stage(r):
        arrive(rx1.at[r], (rs1_sem.at[0, r], rs1_sem.at[1, r]), {"tensor": partner})
        for step in range(1, pairs):
            target = lax.rem(pair + step, pairs)
            tx2[r, step - 1] = (
                part[r, side, target].astype(F32) + rx1[r, target].astype(F32)
            ).astype(BF16)
            send(
                tx2.at[r, step - 1],
                rx2.at[r, step - 1],
                (rs2_sem.at[0, r, step - 1], rs2_sem.at[1, r, step - 1]),
                {"tensor": peer(step)},
            )

    for r in range(2):
        first, last = r * half_blocks, (r + 1) * half_blocks
        key_first, key_last = max(first - 1, 0), min(last + 1, blocks)
        for b in range(first, last):
            for kb in range(key_first, key_last):
                seen = jnp.where(owner[b] == owner[kb], live[kb], 0)
                e_bias[
                    r,
                    (b - first) * BLOCK : (b - first + 1) * BLOCK,
                    (kb - key_first) * BLOCK : (kb - key_first + 1) * BLOCK,
                ] = jnp.where(block_lane < seen, 0.0, RAW_MASKED)
        key_count = (key_last - key_first) * BLOCK
        attend(
            e_q,
            e_k,
            e_v,
            e_bias.at[r, :, pl.ds(0, key_count)],
            e_ctx,
            pl.ds(r * half, half),
            pl.ds(key_first * BLOCK, key_count),
            heads,
        )
        if r == 0:
            loads[4].wait()
        tile = max(256, share)
        per_tile = tile // share
        for index in range(width // tile):
            sums = jnp.dot(
                e_ctx[r * half : (r + 1) * half, :],
                w_eo[:, index * tile : (index + 1) * tile],
                preferred_element_type=F32,
            )
            for inner in range(per_tile):
                j = index * per_tile + inner
                part[r, j % 2, j // 2] = sums[:, inner * share : (inner + 1) * share].astype(
                    BF16
                )
        send(
            part.at[r, 1 - side],
            rx1.at[r],
            (rs1_sem.at[0, r], rs1_sem.at[1, r]),
            {"tensor": partner},
        )
        if r == 0:
            loads[5].wait()
            normalise(dec_v, dec_gain, d_normed, BLOCK)
            second_stage(0)
    loads[6].wait()
    project(d_normed, w_cq, c_q, QUERY_SCALE)
    second_stage(1)

    for step in range(1, groups):
        arrive(
            meta_rx.at[step],
            (meta_sem.at[0, step], meta_sem.at[1, step]),
            {"dp": me_dp},
        )
    for q in range(query_rows // LANES):
        wanted = jnp.broadcast_to(
            query_protein[q : q + 1, :].astype(F32), (LANES, LANES)
        ).T
        for g in range(groups):
            for s in range(slots):
                named = meta_rx[g, s : s + 1, :].astype(F32)
                start = (g * slots + s) * BLOCK
                c_bias[q * LANES : (q + 1) * LANES, start : start + BLOCK] = jnp.where(
                    wanted == named, 0.0, RAW_MASKED
                )

    for r in range(2):
        rows = slice(r * half, (r + 1) * half)
        if share % LANES == 0:
            own = res_v[rows, pl.ds(pl.multiple_of(me_t * share, LANES), share)].astype(F32)
        else:
            own = jnp.zeros((half, share), F32)
            for j in range(tensors):
                mine = jnp.where(me_t == j, 1.0, 0.0)
                own = own + mine * res_v[rows, j * share : (j + 1) * share].astype(F32)
        sums = part[r, side, pair].astype(F32) + rx1[r, pair].astype(F32)
        for step in range(1, pairs):
            arrive(
                rx2.at[r, step - 1],
                (rs2_sem.at[0, r, step - 1], rs2_sem.at[1, r, step - 1]),
                {"tensor": partner},
            )
            sums = sums + rx2[r, step - 1].astype(F32)
        encoded[rows, :] = (own + sums).astype(BF16)

    for g in range(groups):
        for s in range(slots):
            block = jnp.zeros((BLOCK, share), F32)
            for b in range(blocks):
                match = (dest[b] == g) & (rank[b] == s)
                chosen = jnp.where(match, 1.0, 0.0)
                block = block + chosen * encoded[b * BLOCK : (b + 1) * BLOCK, :].astype(F32)
            placed[g, s * BLOCK : (s + 1) * BLOCK, :] = block.astype(BF16)
    for step in range(groups - 1, 0, -1):
        target = lax.rem(me_dp + step, groups)
        send(
            placed.at[target],
            gath.at[groups - step, me_t],
            (a2a_sem.at[0, step], a2a_sem.at[1, groups - step]),
            {"dp": target},
        )
    gath[0, me_t] = placed[me_dp]

    def begin(g):
        if g > 0:
            arrive(
                gath.at[g, me_t], (a2a_sem.at[0, g], a2a_sem.at[1, g]), {"dp": me_dp}
            )
        for step in range(1, pairs):
            send(
                gath.at[g, me_t],
                gath.at[g, me_t],
                (ag_sem.at[0, g, step], ag_sem.at[1, g, step]),
                {"tensor": peer(step)},
            )
        send(
            gath.at[g, me_t],
            gath.at[g, me_t],
            (agp_sem.at[0, g, 0], agp_sem.at[1, g, 0]),
            {"tensor": partner},
        )

    def forward(g):
        for step in range(1, pairs):
            origin = lax.rem(pair + pairs - step, pairs) * 2 + side
            arrive(
                gath.at[g, origin],
                (ag_sem.at[0, g, step], ag_sem.at[1, g, step]),
                {"tensor": partner},
            )
            send(
                gath.at[g, origin],
                gath.at[g, origin],
                (agp_sem.at[0, g, step], agp_sem.at[1, g, step]),
                {"tensor": partner},
            )

    slot_rows = slots * BLOCK

    def keys_values(g):
        for step in range(pairs):
            origin = lax.rem(pair + pairs - step, pairs) * 2 + (1 - side)
            arrive(
                gath.at[g, origin],
                (agp_sem.at[0, g, step], agp_sem.at[1, g, step]),
                {"tensor": partner},
            )
        squares = jnp.zeros((slot_rows, 1), F32)
        for j in range(tensors):
            values = gath[g, j].astype(F32)
            squares = squares + jnp.sum(values * values, axis=1, keepdims=True)
            scaled[:, j * share : (j + 1) * share] = (
                values * final_gain[:, j * share : (j + 1) * share]
            ).astype(BF16)
        key_scale = lax.rsqrt(squares / width + EPSILON)
        project(scaled, w_ck, c_k, key_scale)
        project_values(scaled, w_cv, c_v, key_scale)
        attend_part(
            c_q,
            c_k,
            c_v,
            c_bias.at[:, pl.ds(g * slot_rows, slot_rows)],
            c_tops,
            c_sums,
            c_ctx,
            heads,
            g == 0,
            g == groups - 1,
        )

    loads[7].wait()
    loads[8].wait()
    begin(0)
    for g in range(1, groups + 2):
        if g < groups:
            begin(g)
        if g - 1 < groups:
            forward(g - 1)
        if g >= 2:
            keys_values(g - 2)

    loads[9].wait()
    half_width = width // 2

    def decoder_stage(r):
        arrive(drx1.at[r], (drs1_sem.at[0, r], drs1_sem.at[1, r]), {"tensor": partner})
        for step in range(1, pairs):
            target = lax.rem(pair + step, pairs)
            dtx2[r, step - 1] = (
                dpart[r, side, target].astype(F32) + drx1[r, target].astype(F32)
            ).astype(BF16)
            send(
                dtx2.at[r, step - 1],
                drx2.at[r, step - 1],
                (drs2_sem.at[0, r, step - 1], drs2_sem.at[1, r, step - 1]),
                {"tensor": peer(step)},
            )

    for r in range(2):
        for index in range(half_width // 256):
            start = r * half_width + index * 256
            sums = jnp.dot(
                c_ctx[...], w_co[:, start : start + 256], preferred_element_type=F32
            )
            for j in range(tensors):
                piece = sums[j * row_share : (j + 1) * row_share, :]
                if row_pad > row_share:
                    piece = jnp.concatenate(
                        [piece, jnp.zeros((row_pad - row_share, 256), F32)], axis=0
                    )
                dpart[r, j % 2, j // 2, :, index * 256 : (index + 1) * 256] = piece.astype(
                    BF16
                )
        send(
            dpart.at[r, 1 - side],
            drx1.at[r],
            (drs1_sem.at[0, r], drs1_sem.at[1, r]),
            {"tensor": partner},
        )
    decoder_stage(0)
    decoder_stage(1)
    for r in range(2):
        columns = slice(r * half_width, (r + 1) * half_width)
        if row_share % 16 == 0:
            own = dec_v[pl.ds(pl.multiple_of(me_t * row_share, 16), row_share), columns]
            own = own.astype(F32)
        else:
            own = jnp.zeros((row_share, half_width), F32)
            everything = dec_v[:, columns].astype(F32)
            for j in range(tensors):
                mine = jnp.where(me_t == j, 1.0, 0.0)
                own = own + mine * everything[j * row_share : (j + 1) * row_share, :]
        sums = dpart[r, side, pair].astype(F32) + drx1[r, pair].astype(F32)
        for step in range(1, pairs):
            arrive(
                drx2.at[r, step - 1],
                (drs2_sem.at[0, r, step - 1], drs2_sem.at[1, r, step - 1]),
                {"tensor": partner},
            )
            sums = sums + drx2[r, step - 1].astype(F32)
        decoded[:, columns] = (own + sums[:row_share, :]).astype(BF16)

    for copy in sent:
        copy.wait_send()


def hand_over(first, second, first_out, second_out):
    first_out[...] = first[...]
    second_out[...] = second[...]


def body(groups, tensors, *args):
    (
        residues,
        block_protein,
        protein_length,
        decoder_group,
        enc_gain,
        enc_query,
        enc_key,
        enc_value,
        enc_out,
        decoder_states,
        query_protein,
        dec_gain,
        final_gain,
        cross_query,
        cross_key,
        cross_value,
        cross_out,
    ) = args
    tok_rows, width = residues.shape
    query_rows = decoder_states.shape[0]
    inner = enc_query.shape[1]
    blocks = tok_rows // BLOCK
    slots = blocks // 2
    slot_rows = slots * BLOCK
    pairs = tensors // 2
    half = tok_rows // 2
    share = width // tensors
    row_share = query_rows // tensors
    row_pad = -(-row_share // 16) * 16
    keys = groups * slot_rows
    key_span = min(blocks, blocks // 2 + 1) * BLOCK
    hbm = pl.BlockSpec(memory_space=pl.ANY)
    smem = pl.BlockSpec(memory_space=pltpu.SMEM)
    vmem = pl.BlockSpec(memory_space=pltpu.VMEM)
    weight = pltpu.VMEM((width, inner), BF16)
    out_weight = pltpu.VMEM((inner, width), BF16)
    dma = pltpu.SemaphoreType.DMA
    results = pl.pallas_call(
        functools.partial(kernel, groups, tensors),
        out_shape=(
            jax.ShapeDtypeStruct((tok_rows, share), BF16),
            jax.ShapeDtypeStruct((row_share, width), BF16),
        ),
        in_specs=[
            hbm,
            smem,
            smem,
            smem,
            vmem,
            hbm,
            hbm,
            hbm,
            hbm,
            hbm,
            vmem,
            vmem,
            vmem,
            hbm,
            hbm,
            hbm,
            hbm,
        ],
        out_specs=(vmem, vmem),
        scratch_shapes=[
            pltpu.VMEM((tok_rows, width), BF16),
            pltpu.VMEM((query_rows, width), BF16),
            weight,
            weight,
            weight,
            out_weight,
            weight,
            weight,
            weight,
            out_weight,
            pltpu.VMEM((tok_rows, width), BF16),
            pltpu.VMEM((tok_rows, inner), BF16),
            pltpu.VMEM((tok_rows, inner), BF16),
            pltpu.VMEM((tok_rows, 2 * inner), BF16),
            pltpu.VMEM((tok_rows, inner), BF16),
            pltpu.VMEM((2, half, key_span), F32),
            pltpu.VMEM((2, 2, pairs, half, share), BF16),
            pltpu.VMEM((2, pairs, half, share), BF16),
            pltpu.VMEM((2, pairs - 1, half, share), BF16),
            pltpu.VMEM((2, pairs - 1, half, share), BF16),
            pltpu.VMEM((groups, slot_rows, share), BF16),
            pltpu.VMEM((groups, tensors, slot_rows, share), BF16),
            pltpu.VMEM((groups, 8, LANES), jnp.int32),
            pltpu.VMEM((groups, 8, LANES), jnp.int32),
            pltpu.VMEM((query_rows, width), BF16),
            pltpu.VMEM((query_rows, inner), BF16),
            pltpu.VMEM((slot_rows, inner), BF16),
            pltpu.VMEM((slot_rows, 2 * inner), BF16),
            pltpu.VMEM((query_rows, inner), BF16),
            pltpu.VMEM((query_rows, keys), F32),
            pltpu.VMEM((inner // HEAD_DIM, query_rows, HEAD_DIM), F32),
            pltpu.VMEM((inner // HEAD_DIM, query_rows, 2 * HEAD_DIM), F32),
            pltpu.VMEM((slot_rows, width), BF16),
            pltpu.VMEM((2, 2, pairs, row_pad, width // 2), BF16),
            pltpu.VMEM((2, pairs, row_pad, width // 2), BF16),
            pltpu.VMEM((2, pairs - 1, row_pad, width // 2), BF16),
            pltpu.VMEM((2, pairs - 1, row_pad, width // 2), BF16),
            dma((10,)),
            dma((2, groups)),
            dma((2, 2)),
            dma((2, 2, pairs - 1)),
            dma((2, groups)),
            dma((2, groups, pairs)),
            dma((2, groups, pairs)),
            dma((2, 2)),
            dma((2, 2, pairs - 1)),
        ],
        compiler_params=pltpu.CompilerParams(
            collective_id=0,
            has_side_effects=True,
            vmem_limit_bytes=60 * 1024 * 1024,
        ),
    )(
        residues,
        block_protein,
        protein_length,
        decoder_group,
        enc_gain.reshape(1, width),
        enc_query,
        enc_key,
        enc_value,
        enc_out,
        decoder_states,
        query_protein.reshape(query_rows // LANES, LANES),
        dec_gain.reshape(1, width),
        final_gain.reshape(1, width),
        cross_query,
        cross_key,
        cross_value,
        cross_out,
    )


    return pl.pallas_call(
        hand_over,
        out_shape=tuple(jax.ShapeDtypeStruct(r.shape, r.dtype) for r in results),
        in_specs=[vmem, vmem],
        out_specs=(vmem, vmem),
        compiler_params=pltpu.CompilerParams(vmem_limit_bytes=60 * 1024 * 1024),
    )(*results)


def solution(mesh):
    in_specs = (
        P("dp", None),
        P("dp"),
        P(),
        P(),
        P(),
        P(None, "tensor"),
        P(None, "tensor"),
        P(None, "tensor"),
        P("tensor", None),
        P("dp", None),
        P("dp"),
        P(),
        P(),
        P(None, "tensor"),
        P(None, "tensor"),
        P(None, "tensor"),
        P("tensor", None),
    )
    out_specs = (P("dp", "tensor"), P(("dp", "tensor"), None))
    return jax.shard_map(
        functools.partial(body, mesh.shape["dp"], mesh.shape["tensor"]),
        mesh=mesh,
        in_specs=in_specs,
        out_specs=out_specs,
        check_vma=False,
    )
```
